32 devices in a mesh: member: 2 (over y), gx: 4 (over z), gy: 4 (over x, core).
Axes of the slice: x: 2, y: 2, z: 4, core: 2. Of those that a mesh axis runs over, the one named last changes fastest.
Arguments:
- velocity: float32 [6, 32, 96, 128], P('member', 'gx', 'gy'), parts along dimension 0, may hold values from -6 to 6
- turbine_frame: float32 [4, 4, 8], P('gx', 'gy', 'member'), parts along dimension 2, may hold values from -4 to 128, as said below
- turbine_live: int32 [4, 4, 2], P('gx', 'gy', 'member'), parts along dimension 2, may hold values 0 or 1
- polar_bin: int32 [4, 4, 6, 256], P('gx', 'gy', 'member'), parts along dimension 2, may hold values from 0 to 7
- erosion_id: int32 [4, 4, 6], P('gx', 'gy', 'member'), parts along dimension 2, may hold values from 0 to 15
- polar: float32 [5, 8], replicated, may hold values from 0.01 to 6.5
- erosion: float32 [2, 16], replicated, may hold values from 0.6 to 2
Outputs:
- flow: float32 [6, 32, 96, 128], P('member', 'gx', 'gy'), parts along dimension 0
- blade_load: float32 [4, 4, 6, 3, 256], P('gx', 'gy', 'member'), parts along dimension 2
The draws below stay inside these ranges and needn't reach their ends.
There are 2 independent parts, one for each index of `member`. The reference program is written for one: setup_inputs(seed, part) draws one part's arguments, and reference() takes and returns one part's arrays. A program takes and returns all parts, laid end to end along the dimension named above; an argument that names none is the same for every part. Nothing has to cross between parts.
Inputs may be any that keep to these rules, and one draw needn't show every extreme that they name: turbine_frame holds x in [0, 8), y in [0, 24), z in [8, 120], then an azimuth in [-pi, pi).
All inputs are finite; a program needn't handle non-finite values. No bound on the sum of `turbine_live` on one device may be relied on, other than what follows from the above.
Results may differ from the reference program's by a relative error of at most 0.0003.
The reference program's roundings to bfloat16 on the way count: a program that leaves them out, or rounds other values in their place, can miss the bound.
Values sent between devices are 32-bit elements; how exact they have to be, the bound alone decides.
A program may use at most 64 MiB of HBM per device.

```python
import math
import jax
import jax.numpy as jnp
from jax import lax

CX = 8
CY = 24
NZ = 128
PTS = 256
NSEC = 8
NERO = 16
STEPS = 2
RADIUS = 5
NX = 32
NY = 96
N_GX = 4
N_GY = 4


def draw_turbine_frame(key, part):
    key = jax.random.fold_in(key, 11)
    sub_keys = jax.random.split(key, 4)
    grid_shape = (N_GX, N_GY)
    hub_x = jax.random.uniform(sub_keys[0], grid_shape, jnp.float32, 0.0, CX)
    hub_y = jax.random.uniform(sub_keys[1], grid_shape, jnp.float32, 0.0, CY)
    hub_z = jax.random.uniform(sub_keys[2], grid_shape, jnp.float32, RADIUS + 3.0, NZ - RADIUS - 3.0)
    azimuth = jax.random.uniform(sub_keys[3], grid_shape, jnp.float32, -math.pi, math.pi)
    return jnp.stack([hub_x, hub_y, hub_z, azimuth], axis=-1)


def draw_polar(key, part):
    key = jax.random.fold_in(key, 23)
    lower_end = jnp.array([0.2, 4.0, 0.01, 0.5, 0.3], jnp.float32)
    upper_end = jnp.array([0.6, 6.5, 0.04, 1.5, 1.0], jnp.float32)
    unit_draw = jax.random.uniform(key, (5, NSEC), jnp.float32)
    return lower_end[:, None] + (upper_end - lower_end)[:, None] * unit_draw


def draw_erosion(key, part):
    key = jax.random.fold_in(key, 37)
    lower_end = jnp.array([0.6, 1.0], jnp.float32)
    upper_end = jnp.array([1.0, 2.0], jnp.float32)
    unit_draw = jax.random.uniform(key, (2, NERO), jnp.float32)
    return lower_end[:, None] + (upper_end - lower_end)[:, None] * unit_draw


def plant(values, key, least, top_value):
    longest = values.shape.index(max(values.shape))
    spots = []
    for shift in (0, 1):
        where = [jax.random.randint(jax.random.fold_in(key, axis), (), 0, length) for axis, length in enumerate(values.shape)]
        where[longest] = (where[longest] + shift) % values.shape[longest]
        spots.append(tuple(where))
    return values.at[spots[0]].set(least).at[spots[1]].set(top_value)


def block_scale(rng, shape, pieces, least, high):
    def one(position, shards_of):
        heights = jax.random.uniform(jax.random.fold_in(jax.random.fold_in(rng, 6), position), (shards_of,), jnp.float32, least / len(pieces), high / len(pieces))
        return jnp.repeat(jnp.exp(heights), shape[position] // shards_of).reshape((-1,) + (1,) * (len(shape) - position - 1))

    factor_of = one(*pieces[0])
    for cut in pieces[1:]:
        factor_of = factor_of * one(*cut)
    return factor_of


def noise(rng, extent, scale, most, cuts=(), kind=jnp.bfloat16):
    loudness = block_scale(rng, extent, cuts, -0.22, 0.18) if cuts else 1.0
    entries = jax.random.normal(rng, extent, jnp.float32) * scale * loudness
    return jnp.minimum(jnp.maximum(entries, -most), most).astype(kind)


def setup_inputs(seed: int = 0, part: int = 0) -> dict:
    keys = jax.random.split(jax.random.key(seed), 8)
    part_keys = jax.random.split(jax.random.fold_in(keys[7], part), 8)
    velocity = noise(part_keys[0], (3, NX, NY, NZ), 1.0, 6.0, ((1, 4), (2, 4)), jnp.float32)
    turbine_frame = draw_turbine_frame(jax.random.fold_in(jax.random.fold_in(keys[7], part), 71), part)
    turbine_live = plant((jax.random.randint(part_keys[2], (N_GX, N_GY, 1), 0, 2) < 1).astype(jnp.int32), jax.random.fold_in(part_keys[2], 1), 0, 1)
    polar_bin = plant(jax.random.randint(part_keys[3], (N_GX, N_GY, 3, PTS), 0, NSEC), jax.random.fold_in(part_keys[3], 1), 0, NSEC - 1).astype(jnp.int32)
    erosion_id = plant(jax.random.randint(part_keys[4], (N_GX, N_GY, 3), 0, NERO), jax.random.fold_in(part_keys[4], 1), 0, NERO - 1).astype(jnp.int32)
    polar = draw_polar(jax.random.fold_in(keys[7], 71), part)
    erosion = draw_erosion(jax.random.fold_in(keys[7], 71), part)
    return dict(velocity=velocity, turbine_frame=turbine_frame, turbine_live=turbine_live, polar_bin=polar_bin, erosion_id=erosion_id, polar=polar, erosion=erosion)


TIP_SPEED = 6.0
TIME_STEP = 0.15
BASE_VISCOSITY = 0.1
SMAG_COEF = 0.04
KERNEL_NORM = 35.0 / 96.0
TWIST_RATE = 0.3

def kernel(distance):
    inside = jnp.maximum(1.0 - distance * distance / 9.0, 0.0)
    return KERNEL_NORM * inside * inside * inside

def advance(middle, x_plus, x_minus, y_plus, y_minus, push):
    blank_face = jnp.zeros_like(middle[..., :1])
    z_plus = jnp.concatenate([middle[..., 1:], blank_face], axis=-1)
    z_minus = jnp.concatenate([blank_face, middle[..., :-1]], axis=-1)
    slopes = [(x_plus - x_minus) * 0.5, (y_plus - y_minus) * 0.5, (z_plus - z_minus) * 0.5]
    strain = jnp.zeros_like(middle[0])
    for comp_i in range(3):
        for comp_j in range(3):
            sym_part = 0.5 * (slopes[comp_j][comp_i] + slopes[comp_i][comp_j])
            strain = strain + sym_part * sym_part
    viscosity = BASE_VISCOSITY + SMAG_COEF * jnp.sqrt(2.0 * strain)
    laplace = x_plus + x_minus + y_plus + y_minus + z_plus + z_minus - 6.0 * middle
    carried = middle[0:1] * slopes[0] + middle[1:2] * slopes[1] + middle[2:3] * slopes[2]
    return middle + TIME_STEP * (viscosity[None] * laplace - carried + push)

def blade_geometry(frames, substep):
    point_index = jnp.arange(PTS, dtype=jnp.float32)
    radial = RADIUS * (0.2 + 0.8 * (point_index + 0.5) / PTS)
    phases = jnp.arange(3, dtype=jnp.float32) * (2.0 * math.pi / 3.0)
    turning = TIP_SPEED / RADIUS * TIME_STEP * substep
    azimuth = (frames[..., 3:4] + phases + turning)[..., None]
    cosine = jnp.cos(azimuth)
    sine_value = jnp.sin(azimuth)
    x_point = jnp.broadcast_to(frames[..., 0, None, None], frames.shape[:-1] + (3, PTS))
    y_point = frames[..., 1, None, None] + radial * cosine
    z_point = frames[..., 2, None, None] + radial * sine_value
    return (x_point, y_point, z_point, radial, cosine, sine_value)

def choose(onehot, table_row, trailing):
    return lax.optimization_barrier(jnp.sum(jnp.where(onehot, table_row.reshape((-1,) + (1,) * trailing), 0.0), axis=0))

def blade_forces(sampled, radial, cosine, sine_value, bin_table, wear_ids, alive_flags, polar, erosion):
    section = bin_table[None] == jnp.arange(NSEC, dtype=jnp.int32).reshape((-1,) + (1,) * bin_table.ndim)
    lift_base = choose(section, polar[0], bin_table.ndim)
    lift_slope = choose(section, polar[1], bin_table.ndim)
    drag_base = choose(section, polar[2], bin_table.ndim)
    drag_bend = choose(section, polar[3], bin_table.ndim)
    chord_len = choose(section, polar[4], bin_table.ndim)
    wear_state = wear_ids[None] == jnp.arange(NERO, dtype=jnp.int32).reshape((-1,) + (1,) * wear_ids.ndim)
    lift_wear = choose(wear_state, erosion[0], wear_ids.ndim)[..., None]
    drag_wear = choose(wear_state, erosion[1], wear_ids.ndim)[..., None]
    normal = sampled[..., 0, :]
    swirl_part = cosine * sampled[..., 2, :] - sine_value * sampled[..., 1, :]
    relative = TIP_SPEED / RADIUS * radial - swirl_part
    speed_mag = jnp.sqrt(normal * normal + relative * relative)
    attack = jnp.arctan2(normal, relative) - TWIST_RATE * (1.0 - radial / RADIUS)
    lift_coef = (lift_base + lift_slope * attack) * lift_wear
    drag_coef = (drag_base + drag_bend * attack * attack) * drag_wear
    half_load = 0.5 * chord_len * speed_mag * alive_flags.astype(jnp.float32)[..., None]
    axial = -half_load * (lift_coef * relative + drag_coef * normal)
    spin_load = -half_load * (lift_coef * normal - drag_coef * relative)
    return jnp.stack([axial, -spin_load * sine_value, spin_load * cosine], axis=-2)

def reference(velocity, turbine_frame, turbine_live, polar_bin, erosion_id, polar, erosion):
    slot_count = N_GX * N_GY
    frames = turbine_frame.reshape(slot_count, 4)
    alive_flags = turbine_live.reshape(slot_count, 1)
    bin_table = polar_bin.reshape(slot_count, 3, PTS)
    wear_ids = erosion_id.reshape(slot_count, 3)
    span_x = 6
    span_y = 2 * RADIUS + 6
    span_z = 2 * RADIUS + 6
    anchor = jnp.zeros((), jnp.int32)
    spacing = 0.8 * RADIUS / PTS
    flow_field = velocity
    forces = jnp.zeros((slot_count, 3, 3, PTS), jnp.float32)
    for substep in range(STEPS):
        x_point, y_point, z_point, radial, cosine, sine_value = blade_geometry(frames, substep)
        padded = jnp.pad(flow_field.astype(jnp.bfloat16), ((0, 0), (CX, CX), (CY, CY), (0, 0)), mode='wrap')
        padded = lax.optimization_barrier(padded)

        def slot_window(slot_place):
            place_int = slot_place.astype(jnp.int32)
            frame = frames[place_int]
            low_x = jnp.floor(frame[0]).astype(jnp.int32) - 2
            low_y = jnp.floor(frame[1]).astype(jnp.int32) - RADIUS - 2
            low_z = jnp.clip(jnp.floor(frame[2]).astype(jnp.int32) - RADIUS - 2, 0, NZ - span_z)
            cells_x = low_x.astype(jnp.float32) + jnp.arange(span_x, dtype=jnp.float32)
            cells_y = low_y.astype(jnp.float32) + jnp.arange(span_y, dtype=jnp.float32)
            cells_z = low_z.astype(jnp.float32) + jnp.arange(span_z, dtype=jnp.float32)
            weight_x = kernel(cells_x[:, None, None] - x_point[place_int][None])
            weight_y = kernel(cells_y[:, None, None] - y_point[place_int][None])
            depth_half = kernel(cells_z[:, None, None] - z_point[place_int][None]).astype(jnp.bfloat16)
            depth_half = lax.optimization_barrier(depth_half)
            start = (anchor, place_int // N_GY * CX + CX + low_x, place_int % N_GY * CY + CY + low_y, low_z)
            return (weight_x[:, None] * weight_y[None], depth_half.astype(jnp.float32), start)

        def sample_slot(slot_place):
            weight_xy, weight_z, start = slot_window(slot_place)
            region = lax.dynamic_slice(padded, start, (3, span_x, span_y, span_z)).astype(jnp.float32)
            column_sum = jnp.einsum('cxyz,zbp->cxybp', region, weight_z, precision=lax.Precision.HIGHEST)
            return jnp.einsum('cxybp,xybp->bcp', column_sum, weight_xy, precision=lax.Precision.HIGHEST)
        sampled = lax.map(sample_slot, jnp.arange(slot_count, dtype=jnp.int32))
        forces = blade_forces(sampled, radial, cosine, sine_value, bin_table, wear_ids, alive_flags, polar, erosion)

        def spread_slot(slot_place, grid_push):
            weight_xy, weight_z, start = slot_window(slot_place)
            loads = jnp.transpose(forces[slot_place], (1, 0, 2))
            weighted = (weight_xy[None] * loads[:, None, None] * spacing).astype(jnp.bfloat16)
            weighted = lax.optimization_barrier(weighted).astype(jnp.float32)
            region_push = jnp.einsum('cxybp,zbp->cxyz', weighted, weight_z, precision=lax.Precision.HIGHEST)
            current = lax.dynamic_slice(grid_push, start, region_push.shape)
            return lax.dynamic_update_slice(grid_push, current + region_push, start)
        grid_push = lax.fori_loop(0, slot_count, spread_slot, jnp.zeros((3, NX + 2 * CX, NY + 2 * CY, NZ), jnp.float32))
        folded = grid_push[:, CX:CX + NX]
        folded = folded.at[:, NX - CX:].add(grid_push[:, :CX])
        folded = folded.at[:, :CX].add(grid_push[:, NX + CX:])
        spanwise = folded[:, :, CY:CY + NY]
        spanwise = spanwise.at[:, :, NY - CY:].add(folded[:, :, :CY])
        spanwise = spanwise.at[:, :, :CY].add(folded[:, :, NY + CY:])
        flow_field = advance(flow_field, jnp.roll(flow_field, -1, axis=1), jnp.roll(flow_field, 1, axis=1), jnp.roll(flow_field, -1, axis=2), jnp.roll(flow_field, 1, axis=2), spanwise)
    return (flow_field, (forces / (TIP_SPEED * TIP_SPEED)).reshape(N_GX, N_GY, 3, 3, PTS))
```

```python
import functools
import math

import jax
import jax.numpy as jnp
from jax import lax
from jax.experimental import pallas as pl
from jax.experimental.pallas import tpu as pltpu
from jax.sharding import PartitionSpec as P

PTS = 256
NSEC = 8
NERO = 16
STEPS = 2
RADIUS = 5
BLADES = 3

TIP_SPEED = 6.0
TIME_STEP = 0.15
BASE_VISCOSITY = 0.1
SMAG_COEF = 0.04
KERNEL_NORM = 35.0 / 96.0
TWIST_RATE = 0.3

MARGIN = 8
DEPTH = 16
LANES = 128
POINTS = BLADES * PTS
SPACING = 0.8 * RADIUS / PTS

OFFSETS = [(ox, oy) for ox in (-1, 0, 1) for oy in (-1, 0, 1)]
OTHERS = [o for o in OFFSETS if o != (0, 0)]
F32 = jnp.float32
BF16 = jnp.bfloat16


def slot(offset):
    return (offset[0] + 1) * 3 + offset[1] + 1


def opposite(offset):
    return (-offset[0], -offset[1])


def phi(distance):
    inside = jnp.maximum(1.0 - distance * distance * (1.0 / 9.0), 0.0)
    return KERNEL_NORM * inside * inside * inside


def halves(value):
    high = value.astype(BF16)
    return high, (value - high.astype(F32)).astype(BF16)


def dot(left, right, left_dim, right_dim):
    return lax.dot_general(
        left, right, (((left_dim,), (right_dim,)), ((), ())), preferred_element_type=F32
    )


def per_blade(rows):
    return jnp.concatenate([rows[b : b + 1] for b in range(BLADES)], axis=1)


def planes_of(ox, brick_x):
    if ox < 0:
        return range(0, 3)
    if ox > 0:
        return range(brick_x - 2, brick_x)
    return range(brick_x)


def rows_of(oy, brick_y):
    if oy < 0:
        return (0, MARGIN)
    if oy > 0:
        return (brick_y - MARGIN, brick_y)
    return (0, brick_y)


def window_rows(oy, brick_y):
    if oy < 0:
        return (brick_y + MARGIN, brick_y + 2 * MARGIN)
    if oy > 0:
        return (0, MARGIN)
    return (MARGIN, MARGIN + brick_y)


def step_kernel(
    count_x,
    count_y,
    u_ref,
    frame_ref,
    live_ref,
    bin_ref,
    wear_ref,
    polar_ref,
    erosion_ref,
    flow_ref,
    load_ref,
    pad_ref,
    yface_ref,
    yhalo_ref,
    fsend_ref,
    frames_ref,
    rsend_ref,
    rows_ref,
    gsend_ref,
    push_ref,
    wx_ref,
    pick_ref,
    wy_ref,
    wz_ref,
    base_ref,
    plane_ref,
    fsem,
    rsem,
    gsem,
    xsem,
    ysem,
):
    brick_x, brick_y, height = u_ref.shape[1:]
    width = brick_y + 2 * MARGIN
    me_x = lax.axis_index("gx")
    me_y = lax.axis_index("gy")

    def neighbour(offset):
        return {
            "gx": lax.rem(me_x + (offset[0] + count_x), count_x),
            "gy": lax.rem(me_y + (offset[1] + count_y), count_y),
        }

    def send(src, dst, sems, target, source_slot, target_slot):
        copy = pltpu.make_async_remote_copy(
            src_ref=src,
            dst_ref=dst,
            send_sem=sems.at[0, source_slot],
            recv_sem=sems.at[1, target_slot],
            device_id=neighbour(target),
            device_id_type=pl.DeviceIdType.MESH,
        )
        copy.start()
        return copy

    barrier = pltpu.get_barrier_semaphore()
    for offset in OTHERS:
        pl.semaphore_signal(
            barrier,
            inc=1,
            device_id=neighbour(offset),
            device_id_type=pl.DeviceIdType.MESH,
        )

    hub_x = frame_ref[0, 0, 0]
    hub_y = frame_ref[0, 0, 1]
    hub_z = frame_ref[0, 0, 2]
    phase = frame_ref[0, 0, 3]
    sub8 = lax.broadcasted_iota(jnp.int32, (8, LANES), 0)
    fsend_ref[...] = jnp.where(sub8 == 0, hub_x, hub_z)
    for comp in range(3):
        yface_ref[0, 0, comp] = u_ref[comp, :, 0, :]
        yface_ref[0, 1, comp] = u_ref[comp, :, brick_y - 1, :]
    pl.semaphore_wait(barrier, len(OTHERS))

    sent = []
    frame_copies = {}
    for offset in OTHERS:
        back = opposite(offset)
        frame_copies[back] = send(
            fsend_ref,
            frames_ref.at[slot(back)],
            fsem,
            offset,
            slot(offset),
            slot(back),
        )
    frames_ref[slot((0, 0))] = fsend_ref[...]

    inner = pl.ds(MARGIN, brick_y)

    def send_faces(substep):
        copies = []
        for side, ox in ((0, -1), (1, 1)):
            plane = 0 if side == 0 else brick_x - 1
            halo = brick_x + 1 if side == 0 else 0
            if substep == 0:
                src = u_ref.at[:, plane]
            else:
                src = pad_ref.at[substep, :, plane + 1, inner]
            copies.append(
                send(
                    src,
                    pad_ref.at[substep, :, halo, inner],
                    xsem.at[substep],
                    (ox, 0),
                    side,
                    side,
                )
            )
        for side, oy in ((0, -1), (1, 1)):
            copies.append(
                send(
                    yface_ref.at[substep, side],
                    yhalo_ref.at[substep, side],
                    ysem.at[substep],
                    (0, oy),
                    side,
                    side,
                )
            )
        return copies

    faces = send_faces(0)
    for comp in range(3):
        for x in range(brick_x):
            pad_ref[0, comp, x + 1, MARGIN : MARGIN + brick_y, :] = u_ref[comp, x]

    lane = lax.broadcasted_iota(jnp.int32, (1, POINTS), 1)
    point = (lane % PTS).astype(F32)
    radial = RADIUS * (0.2 + 0.8 * (point + 0.5) / PTS)
    azimuth = jnp.zeros((8, LANES), F32)
    for substep in range(STEPS):
        for blade in range(BLADES):
            angle = phase + blade * (2.0 * math.pi / 3.0)
            angle = angle + TIP_SPEED / RADIUS * TIME_STEP * substep
            azimuth = jnp.where(sub8 == substep * BLADES + blade, angle, azimuth)
    cosines = jnp.cos(azimuth)
    sines = jnp.sin(azimuth)

    def trig_row(table, substep):
        rows = [table[substep * BLADES + b : substep * BLADES + b + 1] for b in range(BLADES)]
        return jnp.concatenate([r for r in rows for _ in range(PTS // LANES)], axis=1)

    cos_rows = [trig_row(cosines, s) for s in range(STEPS)]
    sin_rows = [trig_row(sines, s) for s in range(STEPS)]
    depth_start = jnp.clip(
        jnp.floor(jnp.full((1, LANES), hub_z, F32)) - (RADIUS + 2), 0.0, height - DEPTH
    )[:, 0:1]

    def point_weights(substep):
        y_point = hub_y + radial * cos_rows[substep]
        z_point = hub_z + radial * sin_rows[substep]
        cells_y = lax.broadcasted_iota(jnp.int32, (width, 1), 0).astype(F32) - MARGIN
        wy_ref[substep] = phi(cells_y - y_point)
        cells_z = depth_start + lax.broadcasted_iota(jnp.int32, (DEPTH, 1), 0).astype(F32)
        wz_ref[substep] = phi(cells_z - z_point).astype(BF16)

    for substep in range(STEPS):
        point_weights(substep)

    bins = bin_ref[0, 0]
    tables = []
    for row in range(5):
        table = jnp.zeros((BLADES, PTS), F32)
        for entry in range(NSEC):
            table = jnp.where(bins == entry, polar_ref[row, entry], table)
        tables.append(per_blade(table))
    lift_base, lift_slope, drag_base, drag_bend, chord = tables

    def wear_row(row):
        parts = [
            jnp.full((1, PTS), erosion_ref[row, wear_ref[0, 0, b]], F32) for b in range(BLADES)
        ]
        return jnp.concatenate(parts, axis=1)

    lift_wear = wear_row(0)
    drag_wear = wear_row(1)
    live = live_ref[0, 0, 0].astype(F32)

    x_index = lax.broadcasted_iota(jnp.int32, (brick_x, LANES), 0).astype(F32)
    z_index = lax.broadcasted_iota(jnp.int32, (DEPTH, height), 1).astype(F32)
    k_index = lax.broadcasted_iota(jnp.int32, (DEPTH, height), 0).astype(F32)

    def prepare(offset):
        t = slot(offset)
        wx_ref[t] = phi(x_index - float(offset[0] * brick_x) - frames_ref[t, 0:1, :])
        start = jnp.clip(
            jnp.floor(frames_ref[t, 1:2, :]) - (RADIUS + 2), 0.0, float(height - DEPTH)
        )
        pick_ref[t] = jnp.where(z_index - start == k_index, 1.0, 0.0).astype(BF16)

    def load_half(substep, comp, x, rows):
        cells = pad_ref[substep, comp, x + 1, MARGIN + rows[0] : MARGIN + rows[1], :]
        return cells.astype(BF16).astype(F32)

    def contracted(substep, offset):
        t = slot(offset)
        rows = rows_of(offset[1], brick_y)
        place = window_rows(offset[1], brick_y)
        parts = []
        for comp in range(3):
            total = None
            for x in planes_of(offset[0], brick_x):
                term = wx_ref[t, x : x + 1, :] * load_half(substep, comp, x, rows)
                total = term if total is None else total + term
            if place[0]:
                parts.append(jnp.zeros((place[0], height), F32))
            parts.append(total)
            if width - place[1]:
                parts.append(jnp.zeros((width - place[1], height), F32))
        parts.append(jnp.zeros((LANES - 3 * width, height), F32))
        high, low = halves(jnp.concatenate(parts, axis=0))
        pick = pick_ref[t]
        return dot(pick, high, 1, 1) + dot(pick, low, 1, 1)

    z_lane = lax.broadcasted_iota(jnp.int32, (8, height), 1)

    def stencil(substep, begin, end):
        def one(x, carry):
            for y in range(0, brick_y, 8):
                row = MARGIN + y
                mid, diff, lap = [], [], []
                for c in range(3):
                    m = pad_ref[substep, c, x + 1, row : row + 8, :]
                    xp = pad_ref[substep, c, x + 2, row : row + 8, :]
                    xm = pad_ref[substep, c, x, row : row + 8, :]
                    yp = pad_ref[substep, c, x + 1, row + 1 : row + 9, :]
                    ym = pad_ref[substep, c, x + 1, row - 1 : row + 7, :]
                    zp = jnp.where(z_lane == height - 1, 0.0, pltpu.roll(m, height - 1, 1))
                    zm = jnp.where(z_lane == 0, 0.0, pltpu.roll(m, 1, 1))
                    mid.append(m)
                    diff.append((xp - xm, yp - ym, zp - zm))
                    lap.append(((xp + xm) + (yp + ym)) + ((zp + zm) - 6.0 * m))
                cross = [diff[i][j] + diff[j][i] for i, j in ((0, 1), (0, 2), (1, 2))]
                straight = sum(diff[i][i] * diff[i][i] for i in range(3))
                strain2 = 0.5 * straight + 0.25 * sum(v * v for v in cross)
                visc = BASE_VISCOSITY + SMAG_COEF * jnp.sqrt(strain2)
                for c in range(3):
                    carried = sum(mid[j] * diff[c][j] for j in range(3))
                    base_ref[c, x, y : y + 8, :] = mid[c] + TIME_STEP * (
                        visc * lap[c] - 0.5 * carried
                    )
            return carry

        lax.fori_loop(begin, end, one, 0)

    def place_y_halo(substep):
        for comp in range(3):
            pad_ref[substep, comp, 1 : brick_x + 1, MARGIN + brick_y, :] = yhalo_ref[
                substep, 0, comp
            ]
            pad_ref[substep, comp, 1 : brick_x + 1, MARGIN - 1, :] = yhalo_ref[substep, 1, comp]

    prepare((0, 0))
    for substep in range(STEPS):
        row_copies = {}
        for offset in OTHERS:
            if substep == 0:
                frame_copies[offset].wait_recv()
                prepare(offset)
            t = slot(offset)
            rsend_ref[substep, t] = contracted(substep, offset)
            back = opposite(offset)
            row_copies[back] = send(
                rsend_ref.at[substep, t],
                rows_ref.at[substep, slot(back)],
                rsem.at[substep],
                offset,
                t,
                slot(back),
            )
        if substep > 0:
            faces = send_faces(substep)
        window = contracted(substep, (0, 0))
        for copy in faces:
            copy.wait_recv()
        sent += faces
        place_y_halo(substep)
        stencil(substep, 0, brick_x // 2)

        for offset in OTHERS:
            row_copies[offset].wait_recv()
            window = window + rows_ref[substep, slot(offset)]
        sent += list(row_copies.values())
        high, low = halves(window)
        wz = wz_ref[substep]
        column = dot(high, wz, 0, 0) + dot(low, wz, 0, 0)
        wy = wy_ref[substep]
        velocity = [
            jnp.sum(column[c * width : (c + 1) * width] * wy, axis=0, keepdims=True)
            for c in range(3)
        ]

        cosine, sine = cos_rows[substep], sin_rows[substep]
        normal = velocity[0]
        relative = TIP_SPEED / RADIUS * radial - (cosine * velocity[2] - sine * velocity[1])
        speed = jnp.sqrt(normal * normal + relative * relative)
        attack = jnp.arctan2(normal, relative) - TWIST_RATE * (1.0 - radial / RADIUS)
        lift = (lift_base + lift_slope * attack) * lift_wear
        drag = (drag_base + drag_bend * attack * attack) * drag_wear
        half_load = 0.5 * chord * speed * live
        axial = -half_load * (lift * relative + drag * normal)
        spin = -half_load * (lift * normal - drag * relative)
        force = [axial, -spin * sine, spin * cosine]

        spread = [(wy * (force[c] * SPACING)).astype(BF16) for c in range(3)]
        spread.append(jnp.zeros((LANES - 3 * width, POINTS), BF16))
        gsend_ref[substep] = dot(wz, jnp.concatenate(spread, axis=0), 1, 1)
        push_copies = {}
        for offset in OTHERS:
            back = opposite(offset)
            push_copies[back] = send(
                gsend_ref.at[substep],
                push_ref.at[substep, slot(back)],
                gsem.at[substep],
                offset,
                slot(offset),
                slot(back),
            )
        if substep == STEPS - 1:
            for c in range(3):
                scaled = force[c] * (1.0 / (TIP_SPEED * TIP_SPEED))
                for b in range(BLADES):
                    load_ref[0, 0, b, c : c + 1, :] = scaled[:, b * PTS : (b + 1) * PTS]
        stencil(substep, brick_x // 2, brick_x)

        def expand(offset, part):
            t = slot(offset)
            high, low = halves(part)
            pick = pick_ref[t]
            plane_ref[t] = dot(high, pick, 0, 0) + dot(low, pick, 0, 0)

        expand((0, 0), gsend_ref[substep])
        for offset in OTHERS:
            push_copies[offset].wait_recv()
            expand(offset, push_ref[substep, slot(offset)])
        sent += list(push_copies.values())

        for c in range(3):
            for y in range(0, brick_y, 8):
                for x in range(brick_x):
                    total = None
                    for offset in OFFSETS:
                        rows = rows_of(offset[1], brick_y)
                        if x not in planes_of(offset[0], brick_x):
                            continue
                        if not rows[0] <= y < rows[1]:
                            continue
                        t = slot(offset)
                        row = c * width + window_rows(offset[1], brick_y)[0] + y - rows[0]
                        term = wx_ref[t, x : x + 1, :] * plane_ref[t, row : row + 8, :]
                        total = term if total is None else total + term
                    new = base_ref[c, x, y : y + 8, :] + TIME_STEP * total
                    if substep == STEPS - 1:
                        flow_ref[c, x, y : y + 8, :] = new
                    else:
                        row = MARGIN + y
                        pad_ref[substep + 1, c, x + 1, row : row + 8, :] = new
                        if y == 0:
                            yface_ref[substep + 1, 0, c, x : x + 1, :] = new[0:1]
                        if y == brick_y - 8:
                            yface_ref[substep + 1, 1, c, x : x + 1, :] = new[7:8]

    for copy in list(frame_copies.values()) + sent:
        copy.wait_send()


def body(velocity, turbine_frame, turbine_live, polar_bin, erosion_id, polar, erosion):
    comps, brick_x, brick_y, height = velocity.shape
    width = brick_y + 2 * MARGIN
    vmem = pl.BlockSpec(memory_space=pltpu.VMEM)
    smem = pl.BlockSpec(memory_space=pltpu.SMEM)
    turbines = len(OFFSETS)
    return pl.pallas_call(
        functools.partial(step_kernel, lax.axis_size("gx"), lax.axis_size("gy")),
        out_shape=(
            jax.ShapeDtypeStruct(velocity.shape, F32),
            jax.ShapeDtypeStruct((1, 1, BLADES, 3, PTS), F32),
        ),
        in_specs=[vmem, smem, smem, vmem, smem, smem, smem],
        out_specs=(vmem, vmem),
        scratch_shapes=[
            pltpu.VMEM((STEPS, comps, brick_x + 2, width, height), F32),
            pltpu.VMEM((STEPS, 2, comps, brick_x, height), F32),
            pltpu.VMEM((STEPS, 2, comps, brick_x, height), F32),
            pltpu.VMEM((8, LANES), F32),
            pltpu.VMEM((turbines, 8, LANES), F32),
            pltpu.VMEM((STEPS, turbines, DEPTH, LANES), F32),
            pltpu.VMEM((STEPS, turbines, DEPTH, LANES), F32),
            pltpu.VMEM((STEPS, DEPTH, LANES), F32),
            pltpu.VMEM((STEPS, turbines, DEPTH, LANES), F32),
            pltpu.VMEM((turbines, brick_x, LANES), F32),
            pltpu.VMEM((turbines, DEPTH, height), BF16),
            pltpu.VMEM((STEPS, width, POINTS), F32),
            pltpu.VMEM((STEPS, DEPTH, POINTS), BF16),
            pltpu.VMEM((comps, brick_x, brick_y, height), F32),
            pltpu.VMEM((turbines, LANES, height), F32),
            pltpu.SemaphoreType.DMA((2, turbines)),
            pltpu.SemaphoreType.DMA((STEPS, 2, turbines)),
            pltpu.SemaphoreType.DMA((STEPS, 2, turbines)),
            pltpu.SemaphoreType.DMA((STEPS, 2, 2)),
            pltpu.SemaphoreType.DMA((STEPS, 2, 2)),
        ],
        compiler_params=pltpu.CompilerParams(
            collective_id=0, has_side_effects=True, vmem_limit_bytes=32 * 1024 * 1024
        ),
    )(velocity, turbine_frame, turbine_live, polar_bin, erosion_id, polar, erosion)


def solution(mesh):
    return jax.shard_map(
        body,
        mesh=mesh,
        in_specs=(
            P("member", "gx", "gy", None),
            P("gx", "gy", "member"),
            P("gx", "gy", "member"),
            P("gx", "gy", "member", None),
            P("gx", "gy", "member"),
            P(),
            P(),
        ),
        out_specs=(P("member", "gx", "gy", None), P("gx", "gy", "member", None, None)),
        check_vma=False,
    )
```

```python
import functools
import math

import jax
import jax.numpy as jnp
from jax import lax
from jax.experimental import pallas as pl
from jax.experimental.pallas import tpu as pltpu
from jax.sharding import PartitionSpec as P

PTS = 256
NSEC = 8
NERO = 16
STEPS = 2
RADIUS = 5
BLADES = 3

TIP_SPEED = 6.0
TIME_STEP = 0.15
BASE_VISCOSITY = 0.1
SMAG_COEF = 0.04
KERNEL_NORM = 35.0 / 96.0
TWIST_RATE = 0.3

MARGIN = 8
DEPTH = 16
LANES = 128
POINTS = BLADES * PTS
SPACING = 0.8 * RADIUS / PTS

OFFSETS = [(ox, oy) for ox in (-1, 0, 1) for oy in (-1, 0, 1)]
ACROSS = [(-1, 0), (1, 0), (-1, -1), (-1, 1), (1, -1), (1, 1)]
BESIDE = [(0, -1), (0, 1)]
OTHERS = ACROSS + BESIDE
F32 = jnp.float32
BF16 = jnp.bfloat16


def slot(offset):
    return (offset[0] + 1) * 3 + offset[1] + 1


def opposite(offset):
    return (-offset[0], -offset[1])


def phi(distance):
    inside = jnp.maximum(1.0 - distance * distance * (1.0 / 9.0), 0.0)
    return KERNEL_NORM * inside * inside * inside


def halves(value):
    high = value.astype(BF16)
    return high, (value - high.astype(F32)).astype(BF16)


def dot(left, right, left_dim, right_dim):
    return lax.dot_general(
        left, right, (((left_dim,), (right_dim,)), ((), ())), preferred_element_type=F32
    )


def per_blade(rows):
    return jnp.concatenate([rows[b : b + 1] for b in range(BLADES)], axis=1)


def planes_of(ox, brick_x):
    if ox < 0:
        return range(0, 3)
    if ox > 0:
        return range(brick_x - 2, brick_x)
    return range(brick_x)


def rows_of(oy, brick_y):
    if oy < 0:
        return (0, MARGIN)
    if oy > 0:
        return (brick_y - MARGIN, brick_y)
    return (0, brick_y)


def window_rows(oy, brick_y):
    if oy < 0:
        return (brick_y + MARGIN, brick_y + 2 * MARGIN)
    if oy > 0:
        return (0, MARGIN)
    return (MARGIN, MARGIN + brick_y)


def step_kernel(
    count_x,
    count_y,
    u_hbm,
    frame_hbm,
    live_hbm,
    bin_hbm,
    wear_hbm,
    polar_hbm,
    erosion_hbm,
    flow_ref,
    load_ref,
    pad_ref,
    yface_ref,
    yhalo_ref,
    fsend_ref,
    frames_ref,
    rsend_ref,
    rows_ref,
    gsend_ref,
    push_ref,
    wx_ref,
    pick_ref,
    wy_ref,
    wz_ref,
    base_ref,
    plane_ref,
    frame_ref,
    live_ref,
    bin_ref,
    wear_ref,
    polar_ref,
    erosion_ref,
    load_sem,
    fsem,
    rsem,
    gsem,
    xsem,
    ysem,
):
    brick_x, brick_y, height = u_hbm.shape[1:]
    width = brick_y + 2 * MARGIN
    me_x = lax.axis_index("gx")
    me_y = lax.axis_index("gy")

    def neighbour(offset):
        return {
            "gx": lax.rem(me_x + (offset[0] + count_x), count_x),
            "gy": lax.rem(me_y + (offset[1] + count_y), count_y),
        }

    def send(src, dst, sems, target, source_slot, target_slot):
        copy = pltpu.make_async_remote_copy(
            src_ref=src,
            dst_ref=dst,
            send_sem=sems.at[0, source_slot],
            recv_sem=sems.at[1, target_slot],
            device_id=neighbour(target),
            device_id_type=pl.DeviceIdType.MESH,
        )
        copy.start()
        return copy

    barrier = pltpu.get_barrier_semaphore()
    for offset in OTHERS:
        pl.semaphore_signal(
            barrier,
            inc=1,
            device_id=neighbour(offset),
            device_id_type=pl.DeviceIdType.MESH,
        )

    inner = pl.ds(MARGIN, brick_y)
    fetches = []
    for n, (src, dst) in enumerate(
        (
            (frame_hbm, frame_ref),
            (u_hbm, pad_ref.at[0, :, pl.ds(1, brick_x), inner]),
            (live_hbm, live_ref),
            (bin_hbm, bin_ref),
            (wear_hbm, wear_ref),
            (polar_hbm, polar_ref),
            (erosion_hbm, erosion_ref),
        )
    ):
        fetch = pltpu.make_async_copy(src, dst, load_sem.at[n])
        fetch.start()
        fetches.append(fetch)
    fetches[0].wait()
    hub_x = frame_ref[0, 0, 0]
    hub_y = frame_ref[0, 0, 1]
    hub_z = frame_ref[0, 0, 2]
    phase = frame_ref[0, 0, 3]
    sub8 = lax.broadcasted_iota(jnp.int32, (8, LANES), 0)
    fsend_ref[...] = jnp.where(sub8 == 0, hub_x, hub_z)
    pl.semaphore_wait(barrier, len(OTHERS))

    sent = []
    frame_copies = {}
    for offset in OTHERS:
        back = opposite(offset)
        frame_copies[back] = send(
            fsend_ref,
            frames_ref.at[slot(back)],
            fsem,
            offset,
            slot(offset),
            slot(back),
        )
    frames_ref[slot((0, 0))] = fsend_ref[...]

    def send_faces(substep):
        copies = []
        for side, ox in ((0, -1), (1, 1)):
            plane = 0 if side == 0 else brick_x - 1
            halo = brick_x + 1 if side == 0 else 0
            copies.append(
                send(
                    pad_ref.at[substep, :, plane + 1, inner],
                    pad_ref.at[substep, :, halo, inner],
                    xsem.at[substep],
                    (ox, 0),
                    side,
                    side,
                )
            )
        for side, oy in ((0, -1), (1, 1)):
            copies.append(
                send(
                    yface_ref.at[substep, side],
                    yhalo_ref.at[substep, side],
                    ysem.at[substep],
                    (0, oy),
                    side,
                    side,
                )
            )
        return copies

    for fetch in fetches[1:]:
        fetch.wait()
    for comp in range(3):
        yface_ref[0, 0, comp] = pad_ref[0, comp, 1 : brick_x + 1, MARGIN, :]
        yface_ref[0, 1, comp] = pad_ref[0, comp, 1 : brick_x + 1, MARGIN + brick_y - 1, :]
    faces = send_faces(0)

    lane = lax.broadcasted_iota(jnp.int32, (1, POINTS), 1)
    point = (lane % PTS).astype(F32)
    radial = RADIUS * (0.2 + 0.8 * (point + 0.5) / PTS)
    azimuth = jnp.zeros((8, LANES), F32)
    for substep in range(STEPS):
        for blade in range(BLADES):
            angle = phase + blade * (2.0 * math.pi / 3.0)
            angle = angle + TIP_SPEED / RADIUS * TIME_STEP * substep
            azimuth = jnp.where(sub8 == substep * BLADES + blade, angle, azimuth)
    cosines = jnp.cos(azimuth)
    sines = jnp.sin(azimuth)

    def trig_row(table, substep):
        rows = [table[substep * BLADES + b : substep * BLADES + b + 1] for b in range(BLADES)]
        return jnp.concatenate([r for r in rows for _ in range(PTS // LANES)], axis=1)

    cos_rows = [trig_row(cosines, s) for s in range(STEPS)]
    sin_rows = [trig_row(sines, s) for s in range(STEPS)]
    depth_start = jnp.clip(
        jnp.floor(jnp.full((1, LANES), hub_z, F32)) - (RADIUS + 2), 0.0, height - DEPTH
    )[:, 0:1]

    def point_weights(substep):
        y_point = hub_y + radial * cos_rows[substep]
        z_point = hub_z + radial * sin_rows[substep]
        cells_y = lax.broadcasted_iota(jnp.int32, (width, 1), 0).astype(F32) - MARGIN
        wy_ref[substep] = phi(cells_y - y_point)
        cells_z = depth_start + lax.broadcasted_iota(jnp.int32, (DEPTH, 1), 0).astype(F32)
        wz_ref[substep] = phi(cells_z - z_point).astype(BF16)

    point_weights(0)

    bins = jnp.concatenate([bin_ref[0, b] for b in range(BLADES)], axis=0)
    tables = []
    for row in range(5):
        table = jnp.zeros((BLADES, PTS), F32)
        for entry in range(NSEC):
            table = jnp.where(bins == entry, polar_ref[row, entry], table)
        tables.append(per_blade(table))
    lift_base, lift_slope, drag_base, drag_bend, chord = tables

    def wear_row(row):
        parts = [
            jnp.full((1, PTS), erosion_ref[row, wear_ref[0, 0, b]], F32) for b in range(BLADES)
        ]
        return jnp.concatenate(parts, axis=1)

    lift_wear = wear_row(0)
    drag_wear = wear_row(1)
    live = live_ref[0, 0, 0].astype(F32)

    x_index = lax.broadcasted_iota(jnp.int32, (brick_x, LANES), 0).astype(F32)
    z_index = lax.broadcasted_iota(jnp.int32, (DEPTH, height), 1).astype(F32)
    k_index = lax.broadcasted_iota(jnp.int32, (DEPTH, height), 0).astype(F32)

    def prepare(offset):
        t = slot(offset)
        wx_ref[t] = phi(x_index - float(offset[0] * brick_x) - frames_ref[t, 0:1, :])
        start = jnp.clip(
            jnp.floor(frames_ref[t, 1:2, :]) - (RADIUS + 2), 0.0, float(height - DEPTH)
        )
        pick = jnp.where(z_index - start == k_index, 1.0, 0.0).astype(BF16)
        pick_ref[t] = jnp.concatenate([pick, pick], axis=0)

    def load_half(substep, comp, x, rows):
        cells = pad_ref[substep, comp, x + 1, MARGIN + rows[0] : MARGIN + rows[1], :]
        return cells.astype(BF16).astype(F32)

    def contracted(substep, offset):
        t = slot(offset)
        rows = rows_of(offset[1], brick_y)
        place = window_rows(offset[1], brick_y)
        parts = []
        for comp in range(3):
            total = None
            for x in planes_of(offset[0], brick_x):
                term = wx_ref[t, x : x + 1, :] * load_half(substep, comp, x, rows)
                total = term if total is None else total + term
            if place[0]:
                parts.append(jnp.zeros((place[0], height), F32))
            parts.append(total)
            if width - place[1]:
                parts.append(jnp.zeros((width - place[1], height), F32))
        parts.append(jnp.zeros((LANES - 3 * width, height), F32))
        high, low = halves(jnp.concatenate(parts, axis=0))
        pick = pick_ref[t, 0:DEPTH, :]
        return dot(
            jnp.concatenate([pick, pick], axis=1), jnp.concatenate([high, low], axis=1), 1, 1
        )

    z_lane = lax.broadcasted_iota(jnp.int32, (8, height), 1)

    def stencil(substep, begin, end):
        def one(x, carry):
            for y in range(0, brick_y, 8):
                row = MARGIN + y
                mid, diff, lap = [], [], []
                for c in range(3):
                    m = pad_ref[substep, c, x + 1, row : row + 8, :]
                    xp = pad_ref[substep, c, x + 2, row : row + 8, :]
                    xm = pad_ref[substep, c, x, row : row + 8, :]
                    yp = pad_ref[substep, c, x + 1, row + 1 : row + 9, :]
                    ym = pad_ref[substep, c, x + 1, row - 1 : row + 7, :]
                    zp = jnp.where(z_lane == height - 1, 0.0, pltpu.roll(m, height - 1, 1))
                    zm = jnp.where(z_lane == 0, 0.0, pltpu.roll(m, 1, 1))
                    mid.append(m)
                    diff.append((xp - xm, yp - ym, zp - zm))
                    lap.append(((xp + xm) + (yp + ym)) + ((zp + zm) - 6.0 * m))
                cross = [diff[i][j] + diff[j][i] for i, j in ((0, 1), (0, 2), (1, 2))]
                straight = sum(diff[i][i] * diff[i][i] for i in range(3))
                strain2 = 0.5 * straight + 0.25 * sum(v * v for v in cross)
                visc = BASE_VISCOSITY + SMAG_COEF * jnp.sqrt(strain2)
                for c in range(3):
                    carried = sum(mid[j] * diff[c][j] for j in range(3))
                    base_ref[c, x, y : y + 8, :] = mid[c] + TIME_STEP * (
                        visc * lap[c] - 0.5 * carried
                    )
            return carry

        lax.fori_loop(begin, end, one, 0)

    def place_y_halo(substep):
        for comp in range(3):
            pad_ref[substep, comp, 1 : brick_x + 1, MARGIN + brick_y, :] = yhalo_ref[
                substep, 0, comp
            ]
            pad_ref[substep, comp, 1 : brick_x + 1, MARGIN - 1, :] = yhalo_ref[substep, 1, comp]

    def send_rows(substep, offsets):
        parts = [contracted(substep, offset) for offset in offsets]
        for offset, part in zip(offsets, parts):
            rsend_ref[substep, slot(offset)] = part
        copies = {}
        for offset in offsets:
            back = opposite(offset)
            copies[back] = send(
                rsend_ref.at[substep, slot(offset)],
                rows_ref.at[substep, slot(back)],
                rsem.at[substep],
                offset,
                slot(offset),
                slot(back),
            )
        return copies

    def finish(substep, c, x, y, new):
        if substep == STEPS - 1:
            flow_ref[c, x, y : y + 8, :] = new
        else:
            row = MARGIN + y
            pad_ref[substep + 1, c, x + 1, row : row + 8, :] = new
            if y == 0:
                yface_ref[substep + 1, 0, c, x : x + 1, :] = new[0:1]
            if y == brick_y - 8:
                yface_ref[substep + 1, 1, c, x : x + 1, :] = new[7:8]

    edges = sorted(set(planes_of(-1, brick_x)) | set(planes_of(1, brick_x)))

    def add_push(substep, offsets, planes, last):
        for c in range(3):
            for y in range(0, brick_y, 8):
                for x in planes:
                    total = None
                    for offset in offsets:
                        rows = rows_of(offset[1], brick_y)
                        if x not in planes_of(offset[0], brick_x):
                            continue
                        if not rows[0] <= y < rows[1]:
                            continue
                        t = slot(offset)
                        row = c * width + window_rows(offset[1], brick_y)[0] + y - rows[0]
                        term = wx_ref[t, x : x + 1, :] * plane_ref[t, row : row + 8, :]
                        total = term if total is None else total + term
                    new = base_ref[c, x, y : y + 8, :] + TIME_STEP * total
                    if last or x not in edges:
                        finish(substep, c, x, y, new)
                    else:
                        base_ref[c, x, y : y + 8, :] = new

    prepare((0, 0))
    for substep in range(STEPS):
        row_copies = {}
        if substep == 0:
            for offset in BESIDE:
                frame_copies[offset].wait_recv()
                prepare(offset)
            row_copies.update(send_rows(substep, BESIDE))
            window = contracted(substep, (0, 0))
            for offset in ACROSS:
                frame_copies[offset].wait_recv()
                prepare(offset)
            row_copies.update(send_rows(substep, ACROSS))
        else:
            row_copies.update(send_rows(substep, ACROSS))
            row_copies.update(send_rows(substep, BESIDE))
            faces = send_faces(substep)
            window = contracted(substep, (0, 0))
        sent += faces
        for copy in faces[2:]:
            copy.wait_recv()
        place_y_halo(substep)
        if substep == 0:
            for copy in faces[:2]:
                copy.wait_recv()
            stencil(substep, 0, brick_x)
        else:
            stencil(substep, 1, brick_x - 1)

        for offset in BESIDE + ACROSS:
            row_copies[offset].wait_recv()
            window = window + rows_ref[substep, slot(offset)]
        sent += list(row_copies.values())
        high, low = halves(window)
        wz = wz_ref[substep]
        column = dot(high, wz, 0, 0) + dot(low, wz, 0, 0)
        wy = wy_ref[substep]
        velocity = [
            jnp.sum(column[c * width : (c + 1) * width] * wy, axis=0, keepdims=True)
            for c in range(3)
        ]

        cosine, sine = cos_rows[substep], sin_rows[substep]
        normal = velocity[0]
        relative = TIP_SPEED / RADIUS * radial - (cosine * velocity[2] - sine * velocity[1])
        speed = jnp.sqrt(normal * normal + relative * relative)
        attack = jnp.arctan2(normal, relative) - TWIST_RATE * (1.0 - radial / RADIUS)
        lift = (lift_base + lift_slope * attack) * lift_wear
        drag = (drag_base + drag_bend * attack * attack) * drag_wear
        half_load = 0.5 * chord * speed * live
        axial = -half_load * (lift * relative + drag * normal)
        spin = -half_load * (lift * normal - drag * relative)
        force = [axial, -spin * sine, spin * cosine]

        spread = [(wy * (force[c] * SPACING)).astype(BF16) for c in range(3)]
        spread.append(jnp.zeros((LANES - 3 * width, POINTS), BF16))
        gsend_ref[substep] = dot(wz, jnp.concatenate(spread, axis=0), 1, 1)
        push_copies = {}
        for offset in OTHERS:
            back = opposite(offset)
            push_copies[back] = send(
                gsend_ref.at[substep],
                push_ref.at[substep, slot(back)],
                gsem.at[substep],
                offset,
                slot(offset),
                slot(back),
            )
        if substep == STEPS - 1:
            for c in range(3):
                scaled = force[c] * (1.0 / (TIP_SPEED * TIP_SPEED))
                for b in range(BLADES):
                    load_ref[0, b, c] = scaled[:, b * PTS : (b + 1) * PTS]
        if substep + 1 < STEPS:
            point_weights(substep + 1)
        if substep > 0:
            for copy in faces[:2]:
                copy.wait_recv()
            stencil(substep, 0, 1)
            stencil(substep, brick_x - 1, brick_x)

        def expand(offset, part):
            t = slot(offset)
            high, low = halves(part)
            plane_ref[t] = dot(jnp.concatenate([high, low], axis=0), pick_ref[t], 0, 0)

        expand((0, 0), gsend_ref[substep])
        for offset in BESIDE:
            push_copies[offset].wait_recv()
            expand(offset, push_ref[substep, slot(offset)])
        add_push(substep, [(0, 0)] + BESIDE, range(brick_x), False)
        for offset in ACROSS:
            push_copies[offset].wait_recv()
        for offset in ACROSS:
            expand(offset, push_ref[substep, slot(offset)])
        add_push(substep, ACROSS, edges, True)
        sent += list(push_copies.values())

    for copy in list(frame_copies.values()) + sent:
        copy.wait_send()


def body(velocity, turbine_frame, turbine_live, polar_bin, erosion_id, polar, erosion):
    comps, brick_x, brick_y, height = velocity.shape
    width = brick_y + 2 * MARGIN
    vmem = pl.BlockSpec(memory_space=pltpu.VMEM)
    turbines = len(OFFSETS)
    flow, load = pl.pallas_call(
        functools.partial(step_kernel, lax.axis_size("gx"), lax.axis_size("gy")),
        out_shape=(
            jax.ShapeDtypeStruct(velocity.shape, F32),
            jax.ShapeDtypeStruct((1, BLADES, 3, 1, PTS), F32),
        ),
        in_specs=[pl.BlockSpec(memory_space=pltpu.HBM)] * 7,
        out_specs=(vmem, vmem),
        scratch_shapes=[
            pltpu.VMEM((STEPS, comps, brick_x + 2, width, height), F32),
            pltpu.VMEM((STEPS, 2, comps, brick_x, height), F32),
            pltpu.VMEM((STEPS, 2, comps, brick_x, height), F32),
            pltpu.VMEM((8, LANES), F32),
            pltpu.VMEM((turbines, 8, LANES), F32),
            pltpu.VMEM((STEPS, turbines, DEPTH, LANES), F32),
            pltpu.VMEM((STEPS, turbines, DEPTH, LANES), F32),
            pltpu.VMEM((STEPS, DEPTH, LANES), F32),
            pltpu.VMEM((STEPS, turbines, DEPTH, LANES), F32),
            pltpu.VMEM((turbines, brick_x, LANES), F32),
            pltpu.VMEM((turbines, 2 * DEPTH, height), BF16),
            pltpu.VMEM((STEPS, width, POINTS), F32),
            pltpu.VMEM((STEPS, DEPTH, POINTS), BF16),
            pltpu.VMEM((comps, brick_x, brick_y, height), F32),
            pltpu.VMEM((turbines, LANES, height), F32),
            pltpu.SMEM(turbine_frame.shape, F32),
            pltpu.SMEM(turbine_live.shape, jnp.int32),
            pltpu.VMEM((1, BLADES, 1, PTS), jnp.int32),
            pltpu.SMEM(erosion_id.shape, jnp.int32),
            pltpu.SMEM(polar.shape, F32),
            pltpu.SMEM(erosion.shape, F32),
            pltpu.SemaphoreType.DMA((7,)),
            pltpu.SemaphoreType.DMA((2, turbines)),
            pltpu.SemaphoreType.DMA((STEPS, 2, turbines)),
            pltpu.SemaphoreType.DMA((STEPS, 2, turbines)),
            pltpu.SemaphoreType.DMA((STEPS, 2, 2)),
            pltpu.SemaphoreType.DMA((STEPS, 2, 2)),
        ],
        compiler_params=pltpu.CompilerParams(
            collective_id=0, has_side_effects=True, vmem_limit_bytes=60 * 1024 * 1024
        ),
    )(
        velocity,
        turbine_frame,
        turbine_live,
        jnp.transpose(polar_bin, (0, 2, 1, 3)),
        erosion_id,
        polar,
        erosion,
    )
    return flow, jnp.transpose(load, (0, 3, 1, 2, 4))


def solution(mesh):
    return jax.shard_map(
        body,
        mesh=mesh,
        in_specs=(
            P("member", "gx", "gy", None),
            P("gx", "gy", "member"),
            P("gx", "gy", "member"),
            P("gx", "gy", "member", None),
            P("gx", "gy", "member"),
            P(),
            P(),
        ),
        out_specs=(P("member", "gx", "gy", None), P("gx", "gy", "member", None, None)),
        check_vma=False,
    )
```

```python
import functools
import math

import jax
import jax.numpy as jnp
from jax import lax
from jax.experimental import pallas as pl
from jax.experimental.pallas import tpu as pltpu
from jax.sharding import PartitionSpec as P

PTS = 256
NSEC = 8
NERO = 16
STEPS = 2
RADIUS = 5
BLADES = 3

TIP_SPEED = 6.0
TIME_STEP = 0.15
BASE_VISCOSITY = 0.1
SMAG_COEF = 0.04
KERNEL_NORM = 35.0 / 96.0
TWIST_RATE = 0.3

MARGIN = 8
DEPTH = 16
LANES = 128
POINTS = BLADES * PTS
SPACING = 0.8 * RADIUS / PTS

OFFSETS = [(ox, oy) for ox in (-1, 0, 1) for oy in (-1, 0, 1)]
ACROSS = [(-1, 0), (1, 0), (-1, -1), (-1, 1), (1, -1), (1, 1)]
BESIDE = [(0, -1), (0, 1)]
OTHERS = ACROSS + BESIDE
F32 = jnp.float32
BF16 = jnp.bfloat16


def slot(offset):
    return (offset[0] + 1) * 3 + offset[1] + 1


def opposite(offset):
    return (-offset[0], -offset[1])


def phi(distance):
    inside = jnp.maximum(1.0 - distance * distance * (1.0 / 9.0), 0.0)
    return KERNEL_NORM * inside * inside * inside


def halves(value):
    high = value.astype(BF16)
    return high, (value - high.astype(F32)).astype(BF16)


def dot(left, right, left_dim, right_dim):
    return lax.dot_general(
        left, right, (((left_dim,), (right_dim,)), ((), ())), preferred_element_type=F32
    )


def per_blade(rows):
    return jnp.concatenate([rows[b : b + 1] for b in range(BLADES)], axis=1)


def planes_of(ox, brick_x):
    if ox < 0:
        return range(0, 3)
    if ox > 0:
        return range(brick_x - 2, brick_x)
    return range(brick_x)


def rows_of(oy, brick_y):
    if oy < 0:
        return (0, MARGIN)
    if oy > 0:
        return (brick_y - MARGIN, brick_y)
    return (0, brick_y)


def window_rows(oy, brick_y):
    if oy < 0:
        return (brick_y + MARGIN, brick_y + 2 * MARGIN)
    if oy > 0:
        return (0, MARGIN)
    return (MARGIN, MARGIN + brick_y)


def step_kernel(
    count_x,
    count_y,
    u_hbm,
    frame_hbm,
    live_hbm,
    bin_hbm,
    wear_hbm,
    polar_hbm,
    erosion_hbm,
    flow_ref,
    load_ref,
    pad_ref,
    yface_ref,
    yhalo_ref,
    fsend_ref,
    frames_ref,
    rsend_ref,
    rows_ref,
    gsend_ref,
    push_ref,
    wx_ref,
    pick_ref,
    wy_ref,
    wz_ref,
    base_ref,
    plane_ref,
    frame_ref,
    live_ref,
    bin_ref,
    wear_ref,
    polar_ref,
    erosion_ref,
    load_sem,
    fsem,
    rsem,
    gsem,
    xsem,
    ysem,
):
    brick_x, brick_y, height = u_hbm.shape[1:]
    width = brick_y + 2 * MARGIN
    me_x = lax.axis_index("gx")
    me_y = lax.axis_index("gy")

    along_x = [lax.rem(me_x + (step + count_x), count_x) for step in (-1, 0, 1)]
    along_y = [lax.rem(me_y + (step + count_y), count_y) for step in (-1, 0, 1)]

    def neighbour(offset):
        return {"gx": along_x[offset[0] + 1], "gy": along_y[offset[1] + 1]}

    def send(src, dst, sems, target, source_slot, target_slot):
        copy = pltpu.make_async_remote_copy(
            src_ref=src,
            dst_ref=dst,
            send_sem=sems.at[0, source_slot],
            recv_sem=sems.at[1, target_slot],
            device_id=neighbour(target),
            device_id_type=pl.DeviceIdType.MESH,
        )
        copy.start()
        return copy

    barrier = pltpu.get_barrier_semaphore()
    for offset in OTHERS:
        pl.semaphore_signal(
            barrier,
            inc=1,
            device_id=neighbour(offset),
            device_id_type=pl.DeviceIdType.MESH,
        )

    inner = pl.ds(MARGIN, brick_y)
    fetches = []
    for n, (src, dst) in enumerate(
        (
            (frame_hbm, frame_ref),
            (u_hbm, pad_ref.at[0, :, pl.ds(1, brick_x), inner]),
            (live_hbm, live_ref),
            (bin_hbm, bin_ref),
            (wear_hbm, wear_ref),
            (polar_hbm, polar_ref),
            (erosion_hbm, erosion_ref),
        )
    ):
        fetch = pltpu.make_async_copy(src, dst, load_sem.at[n])
        fetch.start()
        fetches.append(fetch)
    fetches[0].wait()
    hub_x = frame_ref[0, 0, 0]
    hub_y = frame_ref[0, 0, 1]
    hub_z = frame_ref[0, 0, 2]
    phase = frame_ref[0, 0, 3]
    sub8 = lax.broadcasted_iota(jnp.int32, (8, LANES), 0)
    fsend_ref[...] = jnp.where(sub8 == 0, hub_x, hub_z)
    pl.semaphore_wait(barrier, len(OTHERS))

    sent = []
    frame_copies = {}
    for offset in OTHERS:
        back = opposite(offset)
        frame_copies[back] = send(
            fsend_ref,
            frames_ref.at[slot(back)],
            fsem,
            offset,
            slot(offset),
            slot(back),
        )
    frames_ref[slot((0, 0))] = fsend_ref[...]

    def send_faces(substep):
        copies = []
        for side, ox in ((0, -1), (1, 1)):
            plane = 0 if side == 0 else brick_x - 1
            halo = brick_x + 1 if side == 0 else 0
            copies.append(
                send(
                    pad_ref.at[substep, :, plane + 1, inner],
                    pad_ref.at[substep, :, halo, inner],
                    xsem.at[substep],
                    (ox, 0),
                    side,
                    side,
                )
            )
        for side, oy in ((0, -1), (1, 1)):
            copies.append(
                send(
                    yface_ref.at[substep, side],
                    yhalo_ref.at[substep, side],
                    ysem.at[substep],
                    (0, oy),
                    side,
                    side,
                )
            )
        return copies

    for fetch in fetches[1:]:
        fetch.wait()
    for comp in range(3):
        yface_ref[0, 0, comp] = pad_ref[0, comp, 1 : brick_x + 1, MARGIN, :]
        yface_ref[0, 1, comp] = pad_ref[0, comp, 1 : brick_x + 1, MARGIN + brick_y - 1, :]
    faces = send_faces(0)

    lane = lax.broadcasted_iota(jnp.int32, (1, POINTS), 1)
    point = (lane % PTS).astype(F32)
    radial = RADIUS * (0.2 + 0.8 * (point + 0.5) / PTS)
    azimuth = jnp.zeros((8, LANES), F32)
    for substep in range(STEPS):
        for blade in range(BLADES):
            angle = phase + blade * (2.0 * math.pi / 3.0)
            angle = angle + TIP_SPEED / RADIUS * TIME_STEP * substep
            azimuth = jnp.where(sub8 == substep * BLADES + blade, angle, azimuth)
    cosines = jnp.cos(azimuth)
    sines = jnp.sin(azimuth)

    def trig_row(table, substep):
        rows = [table[substep * BLADES + b : substep * BLADES + b + 1] for b in range(BLADES)]
        return jnp.concatenate([r for r in rows for _ in range(PTS // LANES)], axis=1)

    cos_rows = [trig_row(cosines, s) for s in range(STEPS)]
    sin_rows = [trig_row(sines, s) for s in range(STEPS)]
    depth_start = jnp.clip(
        jnp.floor(jnp.full((1, LANES), hub_z, F32)) - (RADIUS + 2), 0.0, height - DEPTH
    )[:, 0:1]

    def point_weights(substep):
        y_point = hub_y + radial * cos_rows[substep]
        z_point = hub_z + radial * sin_rows[substep]
        cells_y = lax.broadcasted_iota(jnp.int32, (width, 1), 0).astype(F32) - MARGIN
        wy_ref[substep] = phi(cells_y - y_point)
        cells_z = depth_start + lax.broadcasted_iota(jnp.int32, (DEPTH, 1), 0).astype(F32)
        depth = phi(cells_z - z_point).astype(BF16)
        wz_ref[substep] = jnp.concatenate([depth, depth], axis=0)

    point_weights(0)

    bins = jnp.concatenate([bin_ref[0, b] for b in range(BLADES)], axis=0)
    tables = []
    for row in range(5):
        table = jnp.zeros((BLADES, PTS), F32)
        for entry in range(NSEC):
            table = jnp.where(bins == entry, polar_ref[row, entry], table)
        tables.append(per_blade(table))
    lift_base, lift_slope, drag_base, drag_bend, chord = tables

    def wear_row(row):
        parts = [
            jnp.full((1, PTS), erosion_ref[row, wear_ref[0, 0, b]], F32) for b in range(BLADES)
        ]
        return jnp.concatenate(parts, axis=1)

    lift_wear = wear_row(0)
    drag_wear = wear_row(1)
    live = live_ref[0, 0, 0].astype(F32)

    x_index = lax.broadcasted_iota(jnp.int32, (brick_x, LANES), 0).astype(F32)
    z_index = lax.broadcasted_iota(jnp.int32, (DEPTH, height), 1).astype(F32)
    k_index = lax.broadcasted_iota(jnp.int32, (DEPTH, height), 0).astype(F32)

    def prepare(offset):
        t = slot(offset)
        wx_ref[t] = phi(x_index - float(offset[0] * brick_x) - frames_ref[t, 0:1, :])
        start = jnp.clip(
            jnp.floor(frames_ref[t, 1:2, :]) - (RADIUS + 2), 0.0, float(height - DEPTH)
        )
        pick = jnp.where(z_index - start == k_index, 1.0, 0.0).astype(BF16)
        pick_ref[t] = jnp.concatenate([pick, pick], axis=0)

    def load_half(substep, comp, x, rows):
        cells = pad_ref[substep, comp, x + 1, MARGIN + rows[0] : MARGIN + rows[1], :]
        return cells.astype(BF16).astype(F32)

    def contracted(substep, offset):
        t = slot(offset)
        rows = rows_of(offset[1], brick_y)
        place = window_rows(offset[1], brick_y)
        parts = []
        for comp in range(3):
            total = None
            for x in planes_of(offset[0], brick_x):
                term = wx_ref[t, x : x + 1, :] * load_half(substep, comp, x, rows)
                total = term if total is None else total + term
            if place[0]:
                parts.append(jnp.zeros((place[0], height), F32))
            parts.append(total)
            if width - place[1]:
                parts.append(jnp.zeros((width - place[1], height), F32))
        parts.append(jnp.zeros((LANES - 3 * width, height), F32))
        high, low = halves(jnp.concatenate(parts, axis=0))
        pick = pick_ref[t, 0:DEPTH, :]
        return dot(
            jnp.concatenate([pick, pick], axis=1), jnp.concatenate([high, low], axis=1), 1, 1
        )

    z_lane = lax.broadcasted_iota(jnp.int32, (8, height), 1)

    def stencil(substep, begin, end):
        def one(x, carry):
            for y in range(0, brick_y, 8):
                row = MARGIN + y
                mid, diff, lap = [], [], []
                for c in range(3):
                    m = pad_ref[substep, c, x + 1, row : row + 8, :]
                    xp = pad_ref[substep, c, x + 2, row : row + 8, :]
                    xm = pad_ref[substep, c, x, row : row + 8, :]
                    yp = pad_ref[substep, c, x + 1, row + 1 : row + 9, :]
                    ym = pad_ref[substep, c, x + 1, row - 1 : row + 7, :]
                    zp = jnp.where(z_lane == height - 1, 0.0, pltpu.roll(m, height - 1, 1))
                    zm = jnp.where(z_lane == 0, 0.0, pltpu.roll(m, 1, 1))
                    mid.append(m)
                    diff.append((xp - xm, yp - ym, zp - zm))
                    lap.append(((xp + xm) + (yp + ym)) + ((zp + zm) - 6.0 * m))
                cross = [diff[i][j] + diff[j][i] for i, j in ((0, 1), (0, 2), (1, 2))]
                straight = sum(diff[i][i] * diff[i][i] for i in range(3))
                strain2 = 0.5 * straight + 0.25 * sum(v * v for v in cross)
                visc = BASE_VISCOSITY + SMAG_COEF * jnp.sqrt(strain2)
                for c in range(3):
                    carried = sum(mid[j] * diff[c][j] for j in range(3))
                    base_ref[c, x, y : y + 8, :] = mid[c] + TIME_STEP * (
                        visc * lap[c] - 0.5 * carried
                    )
            return carry

        lax.fori_loop(begin, end, one, 0)

    def place_y_halo(substep):
        for comp in range(3):
            pad_ref[substep, comp, 1 : brick_x + 1, MARGIN + brick_y, :] = yhalo_ref[
                substep, 0, comp
            ]
            pad_ref[substep, comp, 1 : brick_x + 1, MARGIN - 1, :] = yhalo_ref[substep, 1, comp]

    def send_rows(substep, offsets):
        parts = [contracted(substep, offset) for offset in offsets]
        for offset, part in zip(offsets, parts):
            rsend_ref[substep, slot(offset)] = part
        copies = {}
        for offset in offsets:
            back = opposite(offset)
            copies[back] = send(
                rsend_ref.at[substep, slot(offset)],
                rows_ref.at[substep, slot(back)],
                rsem.at[substep],
                offset,
                slot(offset),
                slot(back),
            )
        return copies

    def finish(substep, c, x, y, new):
        if substep == STEPS - 1:
            flow_ref[c, x, y : y + 8, :] = new
        else:
            row = MARGIN + y
            pad_ref[substep + 1, c, x + 1, row : row + 8, :] = new
            if y == 0:
                yface_ref[substep + 1, 0, c, x : x + 1, :] = new[0:1]
            if y == brick_y - 8:
                yface_ref[substep + 1, 1, c, x : x + 1, :] = new[7:8]

    edges = sorted(set(planes_of(-1, brick_x)) | set(planes_of(1, brick_x)))

    def add_push(substep, offsets, planes, last):
        for c in range(3):
            for y in range(0, brick_y, 8):
                for x in planes:
                    total = None
                    for offset in offsets:
                        rows = rows_of(offset[1], brick_y)
                        if x not in planes_of(offset[0], brick_x):
                            continue
                        if not rows[0] <= y < rows[1]:
                            continue
                        t = slot(offset)
                        row = c * width + window_rows(offset[1], brick_y)[0] + y - rows[0]
                        term = wx_ref[t, x : x + 1, :] * plane_ref[t, row : row + 8, :]
                        total = term if total is None else total + term
                    new = base_ref[c, x, y : y + 8, :] + TIME_STEP * total
                    if last or x not in edges:
                        finish(substep, c, x, y, new)
                    else:
                        base_ref[c, x, y : y + 8, :] = new

    prepare((0, 0))
    for substep in range(STEPS):
        row_copies = {}
        if substep == 0:
            for offset in BESIDE:
                frame_copies[offset].wait_recv()
                prepare(offset)
            row_copies.update(send_rows(substep, BESIDE))
            window = contracted(substep, (0, 0))
            for offset in ACROSS:
                frame_copies[offset].wait_recv()
                prepare(offset)
            row_copies.update(send_rows(substep, ACROSS))
        else:
            row_copies.update(send_rows(substep, ACROSS))
            row_copies.update(send_rows(substep, BESIDE))
            faces = send_faces(substep)
            window = contracted(substep, (0, 0))
        sent += faces
        for copy in faces[2:]:
            copy.wait_recv()
        place_y_halo(substep)
        if substep == 0:
            for copy in faces[:2]:
                copy.wait_recv()
            stencil(substep, 0, brick_x)
        else:
            stencil(substep, 1, brick_x - 1)

        for offset in BESIDE + ACROSS:
            row_copies[offset].wait_recv()
            window = window + rows_ref[substep, slot(offset)]
        sent += list(row_copies.values())
        high, low = halves(window)
        column = dot(jnp.concatenate([high, low], axis=0), wz_ref[substep], 0, 0)
        wz = wz_ref[substep, 0:DEPTH, :]
        wy = wy_ref[substep]
        velocity = [
            jnp.sum(column[c * width : (c + 1) * width] * wy, axis=0, keepdims=True)
            for c in range(3)
        ]

        cosine, sine = cos_rows[substep], sin_rows[substep]
        normal = velocity[0]
        relative = TIP_SPEED / RADIUS * radial - (cosine * velocity[2] - sine * velocity[1])
        speed = jnp.sqrt(normal * normal + relative * relative)
        attack = jnp.arctan2(normal, relative) - TWIST_RATE * (1.0 - radial / RADIUS)
        lift = (lift_base + lift_slope * attack) * lift_wear
        drag = (drag_base + drag_bend * attack * attack) * drag_wear
        half_load = 0.5 * chord * speed * live
        axial = -half_load * (lift * relative + drag * normal)
        spin = -half_load * (lift * normal - drag * relative)
        force = [axial, -spin * sine, spin * cosine]

        spread = [(wy * (force[c] * SPACING)).astype(BF16) for c in range(3)]
        spread.append(jnp.zeros((LANES - 3 * width, POINTS), BF16))
        gsend_ref[substep] = dot(wz, jnp.concatenate(spread, axis=0), 1, 1)
        push_copies = {}
        for offset in OTHERS:
            back = opposite(offset)
            push_copies[back] = send(
                gsend_ref.at[substep],
                push_ref.at[substep, slot(back)],
                gsem.at[substep],
                offset,
                slot(offset),
                slot(back),
            )
        if substep == STEPS - 1:
            for c in range(3):
                scaled = force[c] * (1.0 / (TIP_SPEED * TIP_SPEED))
                for b in range(BLADES):
                    load_ref[0, b, c] = scaled[:, b * PTS : (b + 1) * PTS]
        if substep + 1 < STEPS:
            point_weights(substep + 1)
        if substep > 0:
            for copy in faces[:2]:
                copy.wait_recv()
            stencil(substep, 0, 1)
            stencil(substep, brick_x - 1, brick_x)

        def expand(offset, part):
            t = slot(offset)
            high, low = halves(part)
            plane_ref[t] = dot(jnp.concatenate([high, low], axis=0), pick_ref[t], 0, 0)

        expand((0, 0), gsend_ref[substep])
        for offset in BESIDE:
            push_copies[offset].wait_recv()
            expand(offset, push_ref[substep, slot(offset)])
        add_push(substep, [(0, 0)] + BESIDE, range(brick_x), False)
        for offset in ACROSS:
            push_copies[offset].wait_recv()
        for offset in ACROSS:
            expand(offset, push_ref[substep, slot(offset)])
        add_push(substep, ACROSS, edges, True)
        sent += list(push_copies.values())

    for copy in list(frame_copies.values()) + sent:
        copy.wait_send()


def body(velocity, turbine_frame, turbine_live, polar_bin, erosion_id, polar, erosion):
    comps, brick_x, brick_y, height = velocity.shape
    width = brick_y + 2 * MARGIN
    vmem = pl.BlockSpec(memory_space=pltpu.VMEM)
    turbines = len(OFFSETS)
    flow, load = pl.pallas_call(
        functools.partial(step_kernel, lax.axis_size("gx"), lax.axis_size("gy")),
        out_shape=(
            jax.ShapeDtypeStruct(velocity.shape, F32),
            jax.ShapeDtypeStruct((1, BLADES, 3, 1, PTS), F32),
        ),
        in_specs=[pl.BlockSpec(memory_space=pltpu.HBM)] * 7,
        out_specs=(vmem, vmem),
        scratch_shapes=[
            pltpu.VMEM((STEPS, comps, brick_x + 2, width, height), F32),
            pltpu.VMEM((STEPS, 2, comps, brick_x, height), F32),
            pltpu.VMEM((STEPS, 2, comps, brick_x, height), F32),
            pltpu.VMEM((8, LANES), F32),
            pltpu.VMEM((turbines, 8, LANES), F32),
            pltpu.VMEM((STEPS, turbines, DEPTH, LANES), F32),
            pltpu.VMEM((STEPS, turbines, DEPTH, LANES), F32),
            pltpu.VMEM((STEPS, DEPTH, LANES), F32),
            pltpu.VMEM((STEPS, turbines, DEPTH, LANES), F32),
            pltpu.VMEM((turbines, brick_x, LANES), F32),
            pltpu.VMEM((turbines, 2 * DEPTH, height), BF16),
            pltpu.VMEM((STEPS, width, POINTS), F32),
            pltpu.VMEM((STEPS, 2 * DEPTH, POINTS), BF16),
            pltpu.VMEM((comps, brick_x, brick_y, height), F32),
            pltpu.VMEM((turbines, LANES, height), F32),
            pltpu.SMEM(turbine_frame.shape, F32),
            pltpu.SMEM(turbine_live.shape, jnp.int32),
            pltpu.VMEM((1, BLADES, 1, PTS), jnp.int32),
            pltpu.SMEM(erosion_id.shape, jnp.int32),
            pltpu.SMEM(polar.shape, F32),
            pltpu.SMEM(erosion.shape, F32),
            pltpu.SemaphoreType.DMA((7,)),
            pltpu.SemaphoreType.DMA((2, turbines)),
            pltpu.SemaphoreType.DMA((STEPS, 2, turbines)),
            pltpu.SemaphoreType.DMA((STEPS, 2, turbines)),
            pltpu.SemaphoreType.DMA((STEPS, 2, 2)),
            pltpu.SemaphoreType.DMA((STEPS, 2, 2)),
        ],
        compiler_params=pltpu.CompilerParams(
            collective_id=0, has_side_effects=True, vmem_limit_bytes=54 * 1024 * 1024
        ),
    )(
        velocity,
        turbine_frame,
        turbine_live,
        jnp.transpose(polar_bin, (0, 2, 1, 3)),
        erosion_id,
        polar,
        erosion,
    )
    return flow, jnp.transpose(load, (0, 3, 1, 2, 4))


def solution(mesh):
    return jax.shard_map(
        body,
        mesh=mesh,
        in_specs=(
            P("member", "gx", "gy", None),
            P("gx", "gy", "member"),
            P("gx", "gy", "member"),
            P("gx", "gy", "member", None),
            P("gx", "gy", "member"),
            P(),
            P(),
        ),
        out_specs=(P("member", "gx", "gy", None), P("gx", "gy", "member", None, None)),
        check_vma=False,
    )
```
